32 devices in a mesh: parts: 2 (over y), tm: 4 (over z), tile: 2 (over x), chan: 2 (over core).
Axes of the slice: x: 2, y: 2, z: 4, core: 2. Of those that a mesh axis runs over, the one named last changes fastest.
Arguments:
- pillar_feat: bfloat16 [128, 192, 128], P(('parts', 'tm'), 'tile'), parts along dimension 0, may hold values from -6 to 6
- pillar_cell: int32 [128, 192], P(('parts', 'tm'), 'tile'), parts along dimension 0, may hold values from 0 to 191
- pillar_count: int32 [128, 192], P(('parts', 'tm'), 'tile'), parts along dimension 0, may hold values from 1 to 32
- sweep_embed: bfloat16 [128, 128], P(('parts', 'tm')), parts along dimension 0, may hold values from -3 to 3
- conv_weight: bfloat16 [9, 128, 256], P(None, None, 'chan'), may hold values from -0.5 to 0.5
- proj_weight: bfloat16 [3, 2, 128, 128], P(None, 'chan'), may hold values from -0.5 to 0.5
- d_out: bfloat16 [128, 384, 256], P(('parts', 'tm'), 'tile', 'chan'), parts along dimension 0, may hold values from -0.0390625 to 0.0390625
Outputs:
- attn_out: bfloat16 [128, 384, 256], P(('parts', 'tm'), 'tile', 'chan'), parts along dimension 0
- grad_conv: float32 [9, 256, 256], P(None, 'parts', 'chan'), parts along dimension 1
- grad_proj: float32 [3, 2, 256, 128], P(None, 'chan', 'parts'), parts along dimension 2
The draws below stay inside these ranges and needn't reach their ends.
There are 2 independent parts, one for each index of `parts`. The reference program is written for one: setup_inputs(seed, part) draws one part's arguments, and reference() takes and returns one part's arrays. A program takes and returns all parts, laid end to end along the dimension named above; an argument that names none is the same for every part. Nothing has to cross between parts.
Inputs may be any that keep to these rules, and one draw needn't show every extreme that they name: `pillar_cell`: the cell within the tile's 3 rows of 64 cells, row-major.
All inputs are finite; a program needn't handle non-finite values.
Results may differ from the reference program's by a relative error of at most 0.0069.
Values may be sent and summed in bfloat16 or wider, within the bound.
A program may use at most 64 MiB of HBM per device.

```python
import jax
import jax.numpy as jnp
from jax import lax

C = 128
HD = 128
HEADS = 2
TH = 3
W = 64
PIL_DEV = 96
SWEEPS = 64
CELLS = 384
PILLARS = 192
N_TILE = 2


def touch_ends(values, own_key, least, largest):
    extent = values.shape
    spot = [jax.random.randint(jax.random.fold_in(own_key, axis), (), 0, extent[axis]) for axis in range(len(extent))]
    values = values.at[tuple(spot)].set(least)
    longest = extent.index(max(extent))
    spot[longest] = (spot[longest] + 1) % extent[longest]
    return values.at[tuple(spot)].set(largest)


def block_scale(own_key, extent, split, smallest, largest):
    level = 1.0
    for axis_at, blocks in split:
        steps = jax.random.uniform(jax.random.fold_in(jax.random.fold_in(own_key, 6), axis_at), (blocks,), jnp.float32, smallest / len(split), largest / len(split))
        level = level * jnp.repeat(jnp.exp(steps), extent[axis_at] // blocks).reshape((-1,) + (1,) * (len(extent) - 1 - axis_at))
    return level


def gaussian(key, shape, width, limit, pieces=(), held_as=jnp.bfloat16):
    level = block_scale(key, shape, pieces, -0.22, 0.18) if pieces else 1.0
    values = jax.random.normal(key, shape, jnp.float32) * width * level
    return jnp.minimum(jnp.maximum(values, -limit), limit).astype(held_as)


def setup_inputs(seed: int = 0, part: int = 0) -> dict:
    arg_keys = jax.random.split(jax.random.key(seed), 8)
    part_splits = jax.random.split(jax.random.fold_in(arg_keys[7], part), 8)
    return {
        "pillar_feat": gaussian(part_splits[0], (SWEEPS, PILLARS, C), 1.0, 6.0, ((0, 4), (1, 2))),
        "pillar_cell": touch_ends(jax.random.randint(part_splits[1], (SWEEPS, PILLARS), 0, TH * W), jax.random.fold_in(part_splits[1], 1), 0, (TH * W) - 1).astype(jnp.int32),
        "pillar_count": touch_ends(jax.random.randint(part_splits[2], (SWEEPS, PILLARS), 1, 33), jax.random.fold_in(part_splits[2], 1), 1, 32).astype(jnp.int32),
        "sweep_embed": gaussian(part_splits[3], (SWEEPS, C), 0.5, 3.0, ((0, 4),)),
        "conv_weight": gaussian(arg_keys[4], (9, C, HEADS * HD), C ** -0.5, 0.5, ((2, 2),)),
        "proj_weight": gaussian(arg_keys[5], (3, HEADS, HD, HD), HD ** -0.5, 0.5, ((1, 2),)),
        "d_out": gaussian(part_splits[6], (SWEEPS, CELLS, HEADS * HD), (SWEEPS * CELLS) ** -0.5, 0.0390625, ((0, 4), (1, 2), (2, 2))),
    }


def reverse_cumsum(array_in):
    return jnp.flip(jnp.cumsum(jnp.flip(array_in, 0), 0), 0)


def reference(pillar_feat, pillar_cell, pillar_count, sweep_embed, conv_weight, proj_weight, d_out):
    tile_cells = TH * W
    row_count = TH * N_TILE
    counts_f = pillar_count.astype(jnp.float32)
    count_gate = counts_f / (counts_f + 8.0)
    weighted = pillar_feat.astype(jnp.float32) * count_gate[:, :, None]
    owner_tile = (jnp.arange(PILLARS) // PIL_DEV).astype(jnp.int32)
    target = pillar_cell + owner_tile[None, :] * tile_cells + (jnp.arange(SWEEPS) * CELLS).astype(jnp.int32)[:, None]
    scattered = jax.ops.segment_sum(weighted.reshape(-1, C), target.reshape(-1), num_segments=SWEEPS * CELLS)
    bev_grid = (scattered.reshape(SWEEPS, CELLS, C) + sweep_embed.astype(jnp.float32)[:, None, :]).astype(jnp.bfloat16)
    bev_grid = bev_grid.reshape(SWEEPS, row_count, W, C)
    padded = jnp.pad(bev_grid, ((0, 0), (1, 1), (1, 1), (0, 0)))
    width_out = HEADS * HD
    preact = jnp.zeros((SWEEPS * CELLS, width_out), jnp.float32)
    for offset in range(9):
        row_off = offset // 3
        col_off = offset % 3
        shifted = padded[:, row_off:row_off + row_count, col_off:col_off + W, :].reshape(-1, C)
        preact = preact + jnp.dot(shifted, conv_weight[offset], preferred_element_type=jnp.float32)
    features = jax.nn.silu(preact).astype(jnp.bfloat16).reshape(SWEEPS, CELLS, HEADS, HD)
    feat_f = features.astype(jnp.float32)
    proj_f = proj_weight.astype(jnp.float32)
    query = jnp.einsum("tnhc,hcd->tnhd", feat_f, proj_f[0]).astype(jnp.bfloat16)
    keys = jnp.einsum("tnhc,hcd->tnhd", feat_f, proj_f[1]).astype(jnp.bfloat16)
    values = jnp.einsum("tnhc,hcd->tnhd", feat_f, proj_f[2]).astype(jnp.bfloat16)
    query_f = query.astype(jnp.float32)
    keys_f = keys.astype(jnp.float32)
    values_f = values.astype(jnp.float32)
    scale = 1.0 / ((jnp.arange(SWEEPS) + 1).astype(jnp.float32) * jnp.float32(CELLS))
    pair_sums = jnp.einsum("tnhc,tnhd->thcd", keys_f, values_f)
    kv_state = jnp.cumsum(pair_sums, 0)
    hp = lax.Precision.HIGHEST
    attn_out = (jnp.einsum("tnhc,thcd->tnhd", query_f, kv_state, precision=hp) * scale[:, None, None, None]).astype(jnp.bfloat16)
    scaled_cot = (d_out.astype(jnp.float32).reshape(SWEEPS, CELLS, HEADS, HD) * scale[:, None, None, None]).astype(jnp.bfloat16)
    cot_f = scaled_cot.astype(jnp.float32)
    cot_sums = jnp.einsum("tnhc,tnhd->thcd", query_f, cot_f)
    adjoint = reverse_cumsum(cot_sums)
    grad_query = jnp.einsum("tnhd,thcd->tnhc", cot_f, kv_state, precision=hp).astype(jnp.bfloat16)
    grad_keys = jnp.einsum("tnhd,thcd->tnhc", values_f, adjoint, precision=hp).astype(jnp.bfloat16)
    grad_values = jnp.einsum("tnhc,thcd->tnhd", keys_f, adjoint, precision=hp).astype(jnp.bfloat16)
    gq_f = grad_query.astype(jnp.float32)
    gk_f = grad_keys.astype(jnp.float32)
    gv_f = grad_values.astype(jnp.float32)
    grad_proj = jnp.stack([jnp.einsum("tnhc,tnhd->hcd", feat_f, gq_f), jnp.einsum("tnhc,tnhd->hcd", feat_f, gk_f), jnp.einsum("tnhc,tnhd->hcd", feat_f, gv_f)], 0)
    grad_feat = jnp.einsum("tnhd,hcd->tnhc", gq_f, proj_f[0]) + jnp.einsum("tnhd,hcd->tnhc", gk_f, proj_f[1]) + jnp.einsum("tnhd,hcd->tnhc", gv_f, proj_f[2])
    logistic = 1.0 / (1.0 + jnp.exp(-preact))
    grad_pre = (grad_feat.reshape(-1, width_out) * logistic * (1.0 + preact * (1.0 - logistic))).astype(jnp.bfloat16)
    grad_list = []
    for offset in range(9):
        row_off = offset // 3
        col_off = offset % 3
        shifted = padded[:, row_off:row_off + row_count, col_off:col_off + W, :].reshape(-1, C)
        grad_list.append(jnp.dot(shifted.T, grad_pre, preferred_element_type=jnp.float32))
    grad_conv = jnp.stack(grad_list, 0)
    return attn_out.reshape(SWEEPS, CELLS, width_out), grad_conv, grad_proj
```

```python
import functools

import jax
import jax.numpy as jnp
from jax import lax
from jax.experimental import pallas as pl
from jax.experimental.pallas import tpu as pltpu
from jax.sharding import PartitionSpec as P

W = 64
BF = jnp.bfloat16
F32 = jnp.float32
MESH = pl.DeviceIdType.MESH


def mm(a, b, ca=1, cb=0):
    return lax.dot_general(a, b, (((ca,), (cb,)), ((), ())), preferred_element_type=F32)


def body(
    nm, nt, nsweep, per_tile, band,
    feat, cell, count, embed, wconv, proj, dout,
    attn, gconv, gproj,
    fe, ce, ne, cot, emb, x3, feats, deriv, qkv, kvl, cotl, wqkv, ao, g3, cacc, pacc,
    tks, tkr, zks, zkr, gflat, gsend, grecv, gall,
    pil_s, pil_r, loc, tk_s, tk_r, zk_s, zk_r, att_s, att_r, att_l, gs_s, gs_r, ga_s, ga_r,
):
    group = nm * nt
    cells = nt * band
    width = 128
    tm = lax.axis_index("tm")
    tile = lax.axis_index("tile")
    me = tm * nt + tile

    def peer(d):
        return lax.rem(tile + d, nt)

    def gpeer(d):
        return lax.rem(me + d, group)

    def gid(p):
        return {"tm": p // nt, "tile": lax.rem(p, nt)}

    zkr[...] = jnp.zeros_like(zkr)

    barrier = pltpu.get_barrier_semaphore()

    def greet(d, c):
        pl.semaphore_signal(barrier, inc=1, device_id=gid(gpeer(d)), device_id_type=MESH)
        return c

    lax.fori_loop(1, group, greet, 0)
    mine = pl.ds(tile * nsweep, nsweep)
    locals_ = [
        pltpu.make_async_copy(feat.at[mine], fe.at[:, tile], loc.at[0]),
        pltpu.make_async_copy(cell.at[tile], ce.at[tile], loc.at[1]),
        pltpu.make_async_copy(count.at[tile], ne.at[tile], loc.at[2]),
        pltpu.make_async_copy(dout.at[mine], cot.at[:, tile], loc.at[3]),
    ]
    for c in locals_:
        c.start()
    pl.semaphore_wait(barrier, group - 1)

    def pillar_copy(k, to, here, slot):
        theirs = pl.ds(here * nsweep, nsweep)
        src, dst = (
            lambda: (feat.at[theirs], fe.at[:, slot]),
            lambda: (cell.at[here], ce.at[slot]),
            lambda: (count.at[here], ne.at[slot]),
            lambda: (dout.at[theirs], cot.at[:, slot]),
        )[k]()
        return pltpu.make_async_remote_copy(
            src_ref=src, dst_ref=dst, send_sem=pil_s.at[k, to], recv_sem=pil_r.at[k, slot],
            device_id={"tile": to}, device_id_type=MESH,
        )

    def outgoing(k, to):
        return pillar_copy(k, to, to, tile)

    def arrival(k, frm):
        return pillar_copy(k, frm, tile, frm)

    for d in range(1, nt):
        for k in range(3):
            outgoing(k, peer(d)).start()
    for d in range(1, nt):
        outgoing(3, peer(d)).start()

    for i in range(3):
        wqkv[:, i * width:(i + 1) * width] = proj[i, 0]
    emb[...] = embed[...].astype(F32)
    edge = jnp.zeros((nsweep, W, 3 * width), BF)
    x3[:, 0:W, :] = edge
    x3[:, W + cells:2 * W + cells, :] = edge
    g3[...] = jnp.zeros_like(g3)
    cacc[...] = jnp.zeros_like(cacc)
    pacc[...] = jnp.zeros_like(pacc)

    spot = lax.broadcasted_iota(jnp.int32, (band, per_tile), 0)
    col = lax.rem(lax.broadcasted_iota(jnp.int32, (band, width), 0), W)

    def grid_band(s, j):
        row = ce[j, pl.ds(s, 1), :]
        n = ne[j, pl.ds(s, 1), :].astype(F32)
        gate = n / (n + 8.0)
        full = jnp.where(spot == row, gate, 0.0)
        hi = full.astype(BF)
        lo = (full - hi.astype(F32)).astype(BF)
        values = fe[s, j]
        grid = mm(hi, values) + mm(lo, values) + emb[pl.ds(tile * nsweep + s, 1), :]
        mid = grid.astype(BF)
        grid = mid.astype(F32)
        left = jnp.where(col == 0, 0.0, pltpu.roll(grid, 1, 0)).astype(BF)
        right = jnp.where(col == W - 1, 0.0, pltpu.roll(grid, band - 1, 0)).astype(BF)
        rows = pl.ds(pl.multiple_of(W + j * band, W), band)
        x3[s, rows, 0:width] = left
        x3[s, rows, width:2 * width] = mid
        x3[s, rows, 2 * width:3 * width] = right

    for c in locals_:
        c.wait()

    def own_band(s, c):
        grid_band(s, tile)
        return c

    lax.fori_loop(0, nsweep, own_band, 0)
    for d in range(1, nt):
        for k in range(3):
            arrival(k, peer(d)).wait_recv()

    def forward(s, total):
        for d in range(1, nt):
            grid_band(s, peer(d))
        pre = mm(x3[s, 0:cells, :], wconv[0])
        pre = pre + mm(x3[s, W:W + cells, :], wconv[1])
        pre = pre + mm(x3[s, 2 * W:2 * W + cells, :], wconv[2])
        sig = 1.0 / (1.0 + jnp.exp(-pre))
        f = (pre * sig).astype(BF)
        feats[s] = f
        deriv[s] = sig * (1.0 + pre * (1.0 - sig))
        out = mm(f, wqkv[...]).astype(BF)
        qkv[s] = out
        total = total + mm(out[:, width:2 * width], out[:, 2 * width:], 0, 0)
        kvl[s] = total
        return total

    kv_total = lax.fori_loop(0, nsweep, forward, jnp.zeros((width, width), F32))

    def tile_copy(k, to, slot, sem):
        return pltpu.make_async_remote_copy(
            src_ref=tks.at[k], dst_ref=tkr.at[k, slot], send_sem=tk_s.at[k, to],
            recv_sem=tk_r.at[k, sem], device_id={"tile": to}, device_id_type=MESH,
        )

    def block_copy(k, to, slot, sem):
        return pltpu.make_async_remote_copy(
            src_ref=zks.at[k], dst_ref=zkr.at[k, slot], send_sem=zk_s.at[k, to],
            recv_sem=zk_r.at[k, sem], device_id={"tm": to}, device_id_type=MESH,
        )

    def send_tile(k, total):
        low = total.astype(BF)
        tks[k] = low
        tkr[k, tile] = low
        for d in range(1, nt):
            tile_copy(k, peer(d), tile, tile).start()

    def reaches(k, m):
        return (m > tm) if k == 0 else (m < tm)

    def send_block(k):
        for d in range(1, nt):
            tile_copy(k, peer(d), peer(d), peer(d)).wait_recv()
        block = jnp.zeros((width, width), F32)
        inside = jnp.zeros((width, width), F32)
        for i in range(nt):
            part = tkr[k, i].astype(F32)
            block = block + part
            wanted = (i < tile) if k == 0 else (i > tile)
            inside = inside + jnp.where(wanted, part, 0.0)
        zks[k] = block.astype(BF)
        for m in range(nm):
            @pl.when(reaches(k, m))
            def _():
                block_copy(k, m, tm, tm).start()
        return inside

    def take_block(k, inside):
        for m in range(nm):
            @pl.when(reaches(1 - k, m))
            def _():
                block_copy(k, m, m, m).wait_recv()
        for m in range(nm):
            inside = inside + zkr[k, m].astype(F32)
        return inside

    def scale_of(s):
        t = tm * (nsweep * nt) + tile * nsweep + s + 1
        return 1.0 / (jnp.full((1, width), t, jnp.int32).astype(F32) * float(cells))

    send_tile(0, kv_total)
    for d in range(1, nt):
        arrival(3, peer(d)).wait_recv()
    kv_inside = send_block(0)

    def cot_sum(k, total):
        s = nsweep - 1 - k
        total = total + mm(qkv[s, :, 0:width], cot[s].reshape(cells, width), 0, 0) * scale_of(s)
        cotl[s] = total
        return total

    cot_total = lax.fori_loop(0, nsweep, cot_sum, jnp.zeros((width, width), F32))
    send_tile(1, cot_total)
    before = take_block(0, kv_inside)

    def attn_remote(s, to, slot):
        return pltpu.make_async_remote_copy(
            src_ref=ao.at[s, to], dst_ref=attn.at[slot * nsweep + s], send_sem=att_s.at[s, to],
            recv_sem=att_r.at[s, slot], device_id={"tile": to}, device_id_type=MESH,
        )

    def attn_local(s):
        return pltpu.make_async_copy(ao.at[s, tile], attn.at[tile * nsweep + s], att_l.at[s])

    def attend(s, c):
        state = (before + kvl[s]).astype(BF)
        res = mm(qkv[s, :, 0:width], state) * scale_of(s)
        ao[s] = res.astype(BF).reshape(nt, band, width)
        for d in range(1, nt):
            attn_remote(s, peer(d), tile).start()
        attn_local(s).start()
        return c

    cot_inside = send_block(1)
    lax.fori_loop(0, nsweep, attend, 0)
    after = take_block(1, cot_inside)

    def backward(s, c):
        state = (before + kvl[s]).astype(BF)
        adj = (after + cotl[s]).astype(BF)
        gq = (mm(cot[s].reshape(cells, width), state, 1, 1) * scale_of(s)).astype(BF)
        gk = mm(qkv[s, :, 2 * width:3 * width], adj, 1, 1).astype(BF)
        gv = mm(qkv[s, :, width:2 * width], adj).astype(BF)
        g = jnp.concatenate([gq, gk, gv], axis=1)
        pacc[...] += mm(feats[s], g, 0, 0)
        gp = (mm(g, wqkv[...], 1, 1) * deriv[s]).astype(BF)
        g3[0:cells - W, 0:width] = gp[W:]
        g3[:, width:2 * width] = gp
        g3[W:cells, 2 * width:3 * width] = gp[:cells - W]
        cacc[...] += mm(x3[s, W:W + cells, :], g3[...], 0, 0)
        return c

    lax.fori_loop(0, nsweep, backward, 0)

    nconv = 9 * width
    for a in range(3):
        for b in range(3):
            r = (3 * a + b) * width
            gflat[r:r + width] = cacc[b * width:(b + 1) * width, a * width:(a + 1) * width]
    for i in range(3):
        r = nconv + i * width
        gflat[r:r + width] = pacc[:, i * width:(i + 1) * width]
    extra = gflat.shape[0] - 12 * width
    if extra:
        gflat[12 * width:] = jnp.zeros((extra, width), F32)
    gsend[...] = gflat[...].astype(BF).reshape(gsend.shape)

    def part_copy(p, src, slot):
        return pltpu.make_async_remote_copy(
            src_ref=gsend.at[src], dst_ref=grecv.at[slot], send_sem=gs_s.at[p],
            recv_sem=gs_r.at[slot], device_id=gid(p), device_id_type=MESH,
        )

    def sum_copy(p, slot):
        return pltpu.make_async_remote_copy(
            src_ref=gall.at[slot], dst_ref=gall.at[slot], send_sem=ga_s.at[p],
            recv_sem=ga_r.at[slot], device_id=gid(p), device_id_type=MESH,
        )

    def each(fn, start=1):
        def step(d, c):
            fn(gpeer(d))
            return c
        lax.fori_loop(start, group, step, 0)

    each(lambda p: part_copy(p, p, me).start())

    def add_part(d, total):
        p = gpeer(d)
        part_copy(p, p, p).wait_recv()
        return total + grecv[p].astype(F32)

    total = lax.fori_loop(1, group, add_part, gsend[me].astype(F32))
    gall[me] = total.astype(BF)
    each(lambda p: sum_copy(p, me).start())
    each(lambda p: sum_copy(p, p).wait_recv())
    flat = gall[...].reshape(gflat.shape)
    gconv[...] = flat[0:nconv].astype(F32)
    gproj[...] = flat[nconv:12 * width].astype(F32)

    def drain(s, c):
        for d in range(1, nt):
            attn_remote(s, peer(d), tile).wait_send()
            attn_remote(s, peer(d), peer(d)).wait_recv()
        attn_local(s).wait()
        return c

    lax.fori_loop(0, nsweep, drain, 0)
    for d in range(1, nt):
        for k in range(4):
            outgoing(k, peer(d)).wait_send()
        for k in range(2):
            tile_copy(k, peer(d), tile, tile).wait_send()
    for k in range(2):
        for m in range(nm):
            @pl.when(reaches(k, m))
            def _():
                block_copy(k, m, tm, tm).wait_send()
    each(lambda p: part_copy(p, p, me).wait_send())
    each(lambda p: sum_copy(p, me).wait_send())


def local(nm, nt, feat, cell, count, embed, wconv, proj, dout):
    block, per_tile, width = feat.shape
    band = dout.shape[1]
    nsweep = block // nt
    cells = nt * band
    group = nm * nt
    piece = -(-12 * width // (16 * group)) * 16
    vm = pltpu.VMEM
    dma = pltpu.SemaphoreType.DMA
    vspec = pl.BlockSpec(memory_space=pltpu.VMEM)
    aspec = pl.BlockSpec(memory_space=pl.ANY)
    tokens = nsweep * cells
    out = pl.pallas_call(
        functools.partial(body, nm, nt, nsweep, per_tile, band),
        out_shape=(
            jax.ShapeDtypeStruct((block, band, width), BF),
            jax.ShapeDtypeStruct((9 * width, width), F32),
            jax.ShapeDtypeStruct((3 * width, width), F32),
        ),
        in_specs=[aspec, aspec, aspec, vspec, vspec, vspec, aspec],
        out_specs=(aspec, vspec, vspec),
        scratch_shapes=[
            vm((nsweep, nt, per_tile, width), BF),
            vm((nt, nsweep, per_tile), jnp.int32),
            vm((nt, nsweep, per_tile), jnp.int32),
            vm((nsweep, nt, band, width), BF),
            vm((block, width), F32),
            vm((nsweep, cells + 2 * W, 3 * width), BF),
            vm((nsweep, cells, width), BF),
            vm((nsweep, cells, width), F32),
            vm((nsweep, cells, 3 * width), BF),
            vm((nsweep, width, width), F32),
            vm((nsweep, width, width), F32),
            vm((width, 3 * width), BF),
            vm((nsweep, nt, band, width), BF),
            vm((cells, 3 * width), BF),
            vm((3 * width, 3 * width), F32),
            vm((width, 3 * width), F32),
            vm((2, width, width), BF),
            vm((2, nt, width, width), BF),
            vm((2, width, width), BF),
            vm((2, nm, width, width), BF),
            vm((group * piece, width), F32),
            vm((group, piece, width), BF),
            vm((group, piece, width), BF),
            vm((group, piece, width), BF),
            dma((4, nt)), dma((4, nt)), dma((4,)),
            dma((2, nt)), dma((2, nt)), dma((2, nm)), dma((2, nm)),
            dma((nsweep, nt)), dma((nsweep, nt)), dma((nsweep,)),
            dma((group,)), dma((group,)), dma((group,)), dma((group,)),
        ],
        compiler_params=pltpu.CompilerParams(
            collective_id=0, has_side_effects=True, vmem_limit_bytes=48 * 1024 * 1024
        ),
        cost_estimate=pl.CostEstimate(
            flops=2 * tokens * width * width * 36, bytes_accessed=4 * 1024 * 1024,
            transcendentals=tokens * width,
        ),
    )(
        feat, cell.reshape(nt, nsweep, per_tile), count.reshape(nt, nsweep, per_tile),
        embed, wconv.reshape(3, 3 * width, width), proj, dout,
    )
    return (
        out[0],
        out[1].reshape(9, width, width),
        out[2].reshape(3, 1, width, width),
    )


def solution(mesh):
    return jax.shard_map(
        functools.partial(local, mesh.shape["tm"], mesh.shape["tile"]),
        mesh=mesh,
        in_specs=(
            P(("parts", "tm"), "tile", None),
            P(("parts", "tm"), "tile"),
            P(("parts", "tm"), "tile"),
            P(("parts", "tm"), None),
            P(None, None, "chan"),
            P(None, "chan", None, None),
            P(("parts", "tm"), "tile", "chan"),
        ),
        out_specs=(
            P(("parts", "tm"), "tile", "chan"),
            P(None, "parts", "chan"),
            P(None, "chan", "parts", None),
        ),
        check_vma=False,
    )
```

```python
import functools

import jax
import jax.numpy as jnp
from jax import lax
from jax.experimental import pallas as pl
from jax.experimental.pallas import tpu as pltpu
from jax.sharding import PartitionSpec as P

W = 64
BF = jnp.bfloat16
F32 = jnp.float32
MESH = pl.DeviceIdType.MESH


def mm(a, b, ca=1, cb=0):
    return lax.dot_general(a, b, (((ca,), (cb,)), ((), ())), preferred_element_type=F32)


def body(
    nm, nt, nsweep, per_tile, band,
    feat, cell, count, embed_in, wconv_in, proj_in, dout,
    attn, gconv, gproj,
    embed, wconv, proj, fe, ce, ne, cot, emb, x3, feats, deriv, qkv, kvl, cotl, wqkv, ao, g3, cacc, pacc,
    tks, tkr, zks, zkr, gflat, gsend, grecv, gall,
    pil_s, pil_r, loc, tk_s, tk_r, zk_s, zk_r, att_s, att_r, att_l, gs_s, gs_r, ga_s, ga_r,
):
    group = nm * nt
    cells = nt * band
    width = 128
    tm = lax.axis_index("tm")
    tile = lax.axis_index("tile")
    me = tm * nt + tile

    def peer(d):
        return lax.rem(tile + d, nt)

    def gpeer(d):
        return lax.rem(me + d, group)

    def gid(p):
        return {"tm": p // nt, "tile": lax.rem(p, nt)}

    zkr[...] = jnp.zeros_like(zkr)

    barrier = pltpu.get_barrier_semaphore()

    def greet(d, c):
        pl.semaphore_signal(barrier, inc=1, device_id=gid(gpeer(d)), device_id_type=MESH)
        return c

    lax.fori_loop(1, group, greet, 0)
    mine = pl.ds(tile * nsweep, nsweep)
    locals_ = [
        pltpu.make_async_copy(feat.at[mine], fe.at[:, tile], loc.at[0]),
        pltpu.make_async_copy(cell.at[tile], ce.at[tile], loc.at[1]),
        pltpu.make_async_copy(count.at[tile], ne.at[tile], loc.at[2]),
        pltpu.make_async_copy(embed_in, embed, loc.at[3]),
        pltpu.make_async_copy(wconv_in, wconv, loc.at[4]),
        pltpu.make_async_copy(proj_in, proj, loc.at[5]),
        pltpu.make_async_copy(dout.at[mine], cot.at[:, tile], loc.at[6]),
    ]
    for c in locals_:
        c.start()
    edge = jnp.zeros((nsweep, W, 3 * width), BF)
    x3[:, 0:W, :] = edge
    x3[:, W + cells:2 * W + cells, :] = edge
    g3[...] = jnp.zeros_like(g3)
    cacc[...] = jnp.zeros_like(cacc)
    pacc[...] = jnp.zeros_like(pacc)
    pl.semaphore_wait(barrier, group - 1)

    def pillar_copy(k, to, here, slot):
        theirs = pl.ds(here * nsweep, nsweep)
        src, dst = (
            lambda: (feat.at[theirs], fe.at[:, slot]),
            lambda: (cell.at[here], ce.at[slot]),
            lambda: (count.at[here], ne.at[slot]),
            lambda: (dout.at[theirs], cot.at[:, slot]),
        )[k]()
        return pltpu.make_async_remote_copy(
            src_ref=src, dst_ref=dst, send_sem=pil_s.at[k, to], recv_sem=pil_r.at[k, slot],
            device_id={"tile": to}, device_id_type=MESH,
        )

    def outgoing(k, to):
        return pillar_copy(k, to, to, tile)

    def arrival(k, frm):
        return pillar_copy(k, frm, tile, frm)

    for d in range(1, nt):
        for k in range(3):
            outgoing(k, peer(d)).start()
    for d in range(1, nt):
        outgoing(3, peer(d)).start()


    spot = lax.broadcasted_iota(jnp.int32, (band, per_tile), 0)
    col = lax.rem(lax.broadcasted_iota(jnp.int32, (band, width), 0), W)

    def grid_band(s, j):
        row = ce[j, pl.ds(s, 1), :]
        n = ne[j, pl.ds(s, 1), :].astype(F32)
        gate = n / (n + 8.0)
        full = jnp.where(spot == row, gate, 0.0)
        hi = full.astype(BF)
        lo = (full - hi.astype(F32)).astype(BF)
        values = fe[s, j]
        grid = mm(hi, values) + mm(lo, values) + emb[pl.ds(tile * nsweep + s, 1), :]
        mid = grid.astype(BF)
        grid = mid.astype(F32)
        left = jnp.where(col == 0, 0.0, pltpu.roll(grid, 1, 0)).astype(BF)
        right = jnp.where(col == W - 1, 0.0, pltpu.roll(grid, band - 1, 0)).astype(BF)
        rows = pl.ds(pl.multiple_of(W + j * band, W), band)
        x3[s, rows, 0:width] = left
        x3[s, rows, width:2 * width] = mid
        x3[s, rows, 2 * width:3 * width] = right

    for c in locals_[:6]:
        c.wait()
    for i in range(3):
        wqkv[:, i * width:(i + 1) * width] = proj[i, 0]
    emb[...] = embed[...].astype(F32)

    def own_band(s, c):
        grid_band(s, tile)
        return c

    lax.fori_loop(0, nsweep, own_band, 0)
    for d in range(1, nt):
        for k in range(3):
            arrival(k, peer(d)).wait_recv()

    def forward(s, total):
        for d in range(1, nt):
            grid_band(s, peer(d))
        pre = mm(x3[s, 0:cells, :], wconv[0])
        pre = pre + mm(x3[s, W:W + cells, :], wconv[1])
        pre = pre + mm(x3[s, 2 * W:2 * W + cells, :], wconv[2])
        sig = 1.0 / (1.0 + jnp.exp(-pre))
        f = (pre * sig).astype(BF)
        feats[s] = f
        deriv[s] = sig * (1.0 + pre * (1.0 - sig))
        out = mm(f, wqkv[...]).astype(BF)
        qkv[s] = out
        total = total + mm(out[:, width:2 * width], out[:, 2 * width:], 0, 0)
        kvl[s] = total
        return total

    kv_total = lax.fori_loop(0, nsweep, forward, jnp.zeros((width, width), F32))

    def tile_copy(k, to, slot, sem):
        return pltpu.make_async_remote_copy(
            src_ref=tks.at[k], dst_ref=tkr.at[k, slot], send_sem=tk_s.at[k, to],
            recv_sem=tk_r.at[k, sem], device_id={"tile": to}, device_id_type=MESH,
        )

    def block_copy(k, to, slot, sem):
        return pltpu.make_async_remote_copy(
            src_ref=zks.at[k], dst_ref=zkr.at[k, slot], send_sem=zk_s.at[k, to],
            recv_sem=zk_r.at[k, sem], device_id={"tm": to}, device_id_type=MESH,
        )

    def send_tile(k, total):
        low = total.astype(BF)
        tks[k] = low
        tkr[k, tile] = low
        for d in range(1, nt):
            tile_copy(k, peer(d), tile, tile).start()

    def reaches(k, m):
        return (m > tm) if k == 0 else (m < tm)

    def send_block(k):
        for d in range(1, nt):
            tile_copy(k, peer(d), peer(d), peer(d)).wait_recv()
        block = jnp.zeros((width, width), F32)
        inside = jnp.zeros((width, width), F32)
        for i in range(nt):
            part = tkr[k, i].astype(F32)
            block = block + part
            wanted = (i < tile) if k == 0 else (i > tile)
            inside = inside + jnp.where(wanted, part, 0.0)
        zks[k] = block.astype(BF)
        for m in range(nm):
            @pl.when(reaches(k, m))
            def _():
                block_copy(k, m, tm, tm).start()
        return inside

    def take_block(k, inside):
        for m in range(nm):
            @pl.when(reaches(1 - k, m))
            def _():
                block_copy(k, m, m, m).wait_recv()
        for m in range(nm):
            inside = inside + zkr[k, m].astype(F32)
        return inside

    def scale_of(s):
        t = tm * (nsweep * nt) + tile * nsweep + s + 1
        return 1.0 / (jnp.full((1, width), t, jnp.int32).astype(F32) * float(cells))

    send_tile(0, kv_total)
    kv_inside = send_block(0)
    locals_[6].wait()
    for d in range(1, nt):
        arrival(3, peer(d)).wait_recv()

    def cot_sum(k, total):
        s = nsweep - 1 - k
        total = total + mm(qkv[s, :, 0:width], cot[s].reshape(cells, width), 0, 0) * scale_of(s)
        cotl[s] = total
        return total

    cot_total = lax.fori_loop(0, nsweep, cot_sum, jnp.zeros((width, width), F32))
    send_tile(1, cot_total)
    before = take_block(0, kv_inside)

    def attn_remote(s, to, slot):
        return pltpu.make_async_remote_copy(
            src_ref=ao.at[s, to], dst_ref=attn.at[slot * nsweep + s], send_sem=att_s.at[s, to],
            recv_sem=att_r.at[s, slot], device_id={"tile": to}, device_id_type=MESH,
        )

    def attn_local(s):
        return pltpu.make_async_copy(ao.at[s, tile], attn.at[tile * nsweep + s], att_l.at[s])

    def attend(s, c):
        state = (before + kvl[s]).astype(BF)
        res = mm(qkv[s, :, 0:width], state) * scale_of(s)
        ao[s] = res.astype(BF).reshape(nt, band, width)
        for d in range(1, nt):
            attn_remote(s, peer(d), tile).start()
        attn_local(s).start()
        return c

    cot_inside = send_block(1)
    lax.fori_loop(0, nsweep, attend, 0)
    after = take_block(1, cot_inside)

    def backward(s, c):
        state = (before + kvl[s]).astype(BF)
        adj = (after + cotl[s]).astype(BF)
        gq = (mm(cot[s].reshape(cells, width), state, 1, 1) * scale_of(s)).astype(BF)
        gk = mm(qkv[s, :, 2 * width:3 * width], adj, 1, 1).astype(BF)
        gv = mm(qkv[s, :, width:2 * width], adj).astype(BF)
        g = jnp.concatenate([gq, gk, gv], axis=1)
        pacc[...] += mm(feats[s], g, 0, 0)
        gp = (mm(g, wqkv[...], 1, 1) * deriv[s]).astype(BF)
        g3[0:cells - W, 0:width] = gp[W:]
        g3[:, width:2 * width] = gp
        g3[W:cells, 2 * width:3 * width] = gp[:cells - W]
        cacc[...] += mm(x3[s, W:W + cells, :], g3[...], 0, 0)
        return c

    lax.fori_loop(0, nsweep, backward, 0)

    nconv = 9 * width
    for a in range(3):
        for b in range(3):
            r = (3 * a + b) * width
            gflat[r:r + width] = cacc[b * width:(b + 1) * width, a * width:(a + 1) * width]
    for i in range(3):
        r = nconv + i * width
        gflat[r:r + width] = pacc[:, i * width:(i + 1) * width]
    extra = gflat.shape[0] - 12 * width
    if extra:
        gflat[12 * width:] = jnp.zeros((extra, width), F32)
    gsend[...] = gflat[...].astype(BF).reshape(gsend.shape)

    def part_copy(p, src, slot):
        return pltpu.make_async_remote_copy(
            src_ref=gsend.at[src], dst_ref=grecv.at[slot], send_sem=gs_s.at[p],
            recv_sem=gs_r.at[slot], device_id=gid(p), device_id_type=MESH,
        )

    def sum_copy(p, slot):
        return pltpu.make_async_remote_copy(
            src_ref=gall.at[slot], dst_ref=gall.at[slot], send_sem=ga_s.at[p],
            recv_sem=ga_r.at[slot], device_id=gid(p), device_id_type=MESH,
        )

    def each(fn, start=1):
        def step(d, c):
            fn(gpeer(d))
            return c
        lax.fori_loop(start, group, step, 0)

    each(lambda p: part_copy(p, p, me).start())

    def add_part(d, total):
        p = gpeer(d)
        part_copy(p, p, p).wait_recv()
        return total + grecv[p].astype(F32)

    total = lax.fori_loop(1, group, add_part, gsend[me].astype(F32))
    gall[me] = total.astype(BF)
    each(lambda p: sum_copy(p, me).start())
    each(lambda p: sum_copy(p, p).wait_recv())
    flat = gall[...].reshape(gflat.shape)
    gconv[...] = flat[0:nconv].astype(F32)
    gproj[...] = flat[nconv:12 * width].astype(F32)

    def drain(s, c):
        for d in range(1, nt):
            attn_remote(s, peer(d), tile).wait_send()
            attn_remote(s, peer(d), peer(d)).wait_recv()
        attn_local(s).wait()
        return c

    lax.fori_loop(0, nsweep, drain, 0)
    for d in range(1, nt):
        for k in range(4):
            outgoing(k, peer(d)).wait_send()
        for k in range(2):
            tile_copy(k, peer(d), tile, tile).wait_send()
    for k in range(2):
        for m in range(nm):
            @pl.when(reaches(k, m))
            def _():
                block_copy(k, m, tm, tm).wait_send()
    each(lambda p: part_copy(p, p, me).wait_send())
    each(lambda p: sum_copy(p, me).wait_send())


def local(nm, nt, feat, cell, count, embed, wconv, proj, dout):
    block, per_tile, width = feat.shape
    band = dout.shape[1]
    nsweep = block // nt
    cells = nt * band
    group = nm * nt
    piece = -(-12 * width // (16 * group)) * 16
    vm = pltpu.VMEM
    dma = pltpu.SemaphoreType.DMA
    vspec = pl.BlockSpec(memory_space=pltpu.VMEM)
    aspec = pl.BlockSpec(memory_space=pl.ANY)
    hspec = pl.BlockSpec(memory_space=pltpu.HBM)
    tokens = nsweep * cells
    out = pl.pallas_call(
        functools.partial(body, nm, nt, nsweep, per_tile, band),
        out_shape=(
            jax.ShapeDtypeStruct((block, band, width), BF),
            jax.ShapeDtypeStruct((9 * width, width), F32),
            jax.ShapeDtypeStruct((3 * width, width), F32),
        ),
        in_specs=[hspec] * 7,
        out_specs=(aspec, vspec, vspec),
        scratch_shapes=[
            vm((block, width), BF),
            vm((3, 3 * width, width), BF),
            vm((3, 1, width, width), BF),
            vm((nsweep, nt, per_tile, width), BF),
            vm((nt, nsweep, per_tile), jnp.int32),
            vm((nt, nsweep, per_tile), jnp.int32),
            vm((nsweep, nt, band, width), BF),
            vm((block, width), F32),
            vm((nsweep, cells + 2 * W, 3 * width), BF),
            vm((nsweep, cells, width), BF),
            vm((nsweep, cells, width), F32),
            vm((nsweep, cells, 3 * width), BF),
            vm((nsweep, width, width), F32),
            vm((nsweep, width, width), F32),
            vm((width, 3 * width), BF),
            vm((nsweep, nt, band, width), BF),
            vm((cells, 3 * width), BF),
            vm((3 * width, 3 * width), F32),
            vm((width, 3 * width), F32),
            vm((2, width, width), BF),
            vm((2, nt, width, width), BF),
            vm((2, width, width), BF),
            vm((2, nm, width, width), BF),
            vm((group * piece, width), F32),
            vm((group, piece, width), BF),
            vm((group, piece, width), BF),
            vm((group, piece, width), BF),
            dma((4, nt)), dma((4, nt)), dma((7,)),
            dma((2, nt)), dma((2, nt)), dma((2, nm)), dma((2, nm)),
            dma((nsweep, nt)), dma((nsweep, nt)), dma((nsweep,)),
            dma((group,)), dma((group,)), dma((group,)), dma((group,)),
        ],
        compiler_params=pltpu.CompilerParams(
            collective_id=0, has_side_effects=True, vmem_limit_bytes=65000 * 1024
        ),
        cost_estimate=pl.CostEstimate(
            flops=2 * tokens * width * width * 36, bytes_accessed=4 * 1024 * 1024,
            transcendentals=tokens * width,
        ),
    )(
        feat, cell.reshape(nt, nsweep, per_tile), count.reshape(nt, nsweep, per_tile),
        embed, wconv.reshape(3, 3 * width, width), proj, dout,
    )
    return (
        out[0],
        out[1].reshape(9, width, width),
        out[2].reshape(3, 1, width, width),
    )


def solution(mesh):
    return jax.shard_map(
        functools.partial(local, mesh.shape["tm"], mesh.shape["tile"]),
        mesh=mesh,
        in_specs=(
            P(("parts", "tm"), "tile", None),
            P(("parts", "tm"), "tile"),
            P(("parts", "tm"), "tile"),
            P(("parts", "tm"), None),
            P(None, None, "chan"),
            P(None, "chan", None, None),
            P(("parts", "tm"), "tile", "chan"),
        ),
        out_specs=(
            P(("parts", "tm"), "tile", "chan"),
            P(None, "parts", "chan"),
            P(None, "chan", "parts", None),
        ),
        check_vma=False,
    )
```

```python
import functools

import jax
import jax.numpy as jnp
from jax import lax
from jax.experimental import pallas as pl
from jax.experimental.pallas import tpu as pltpu
from jax.sharding import PartitionSpec as P

W = 64
BF = jnp.bfloat16
F32 = jnp.float32
MESH = pl.DeviceIdType.MESH


def mm(a, b, ca=1, cb=0):
    return lax.dot_general(a, b, (((ca,), (cb,)), ((), ())), preferred_element_type=F32)


def body(
    nm, nt, nsweep, per_tile, band,
    feat, cell, count, embed_in, wconv_in, proj_in, dout,
    attn, gconv, gproj,
    embed, wconv, proj, fe, ce, ne, cot, emb, x3, feats, gqs, deriv, qkv, kvl, cotl, wqkv, ao, g3, cacc, pacc,
    tks, tkr, zks, zkr, gflat, gsend, grecv, gall,
    pil_s, pil_r, loc, tk_s, tk_r, zk_s, zk_r, att_s, att_r, att_l, gs_s, gs_r, ga_s, ga_r,
):
    group = nm * nt
    cells = nt * band
    width = 128
    tm = lax.axis_index("tm")
    tile = lax.axis_index("tile")
    me = tm * nt + tile

    def peer(d):
        return lax.rem(tile + d, nt)

    def gpeer(d):
        return lax.rem(me + d, group)

    def gid(p):
        return {"tm": p // nt, "tile": lax.rem(p, nt)}

    zkr[...] = jnp.zeros_like(zkr)

    barrier = pltpu.get_barrier_semaphore()

    def greet(d, c):
        pl.semaphore_signal(barrier, inc=1, device_id=gid(gpeer(d)), device_id_type=MESH)
        return c

    lax.fori_loop(1, group, greet, 0)
    mine = pl.ds(tile * nsweep, nsweep)
    locals_ = [
        pltpu.make_async_copy(feat.at[mine], fe.at[:, tile], loc.at[0]),
        pltpu.make_async_copy(cell.at[tile], ce.at[tile], loc.at[1]),
        pltpu.make_async_copy(count.at[tile], ne.at[tile], loc.at[2]),
        pltpu.make_async_copy(embed_in, embed, loc.at[3]),
        pltpu.make_async_copy(wconv_in, wconv, loc.at[4]),
        pltpu.make_async_copy(proj_in, proj, loc.at[5]),
        pltpu.make_async_copy(dout.at[mine], cot.at[:, tile], loc.at[6]),
    ]
    for c in locals_:
        c.start()
    edge = jnp.zeros((nsweep, W, 3 * width), BF)
    x3[:, 0:W, :] = edge
    x3[:, W + cells:2 * W + cells, :] = edge
    g3[...] = jnp.zeros_like(g3)
    cacc[...] = jnp.zeros_like(cacc)
    pacc[...] = jnp.zeros_like(pacc)
    pl.semaphore_wait(barrier, group - 1)

    def pillar_copy(k, to, here, slot):
        theirs = pl.ds(here * nsweep, nsweep)
        src, dst = (
            lambda: (feat.at[theirs], fe.at[:, slot]),
            lambda: (cell.at[here], ce.at[slot]),
            lambda: (count.at[here], ne.at[slot]),
            lambda: (dout.at[theirs], cot.at[:, slot]),
        )[k]()
        return pltpu.make_async_remote_copy(
            src_ref=src, dst_ref=dst, send_sem=pil_s.at[k, to], recv_sem=pil_r.at[k, slot],
            device_id={"tile": to}, device_id_type=MESH,
        )

    def outgoing(k, to):
        return pillar_copy(k, to, to, tile)

    def arrival(k, frm):
        return pillar_copy(k, frm, tile, frm)

    for d in range(1, nt):
        for k in range(3):
            outgoing(k, peer(d)).start()


    spot = lax.broadcasted_iota(jnp.int32, (band, per_tile), 0)
    col = lax.rem(lax.broadcasted_iota(jnp.int32, (band, width), 0), W)

    def grid_band(s, j):
        row = ce[j, pl.ds(s, 1), :]
        n = ne[j, pl.ds(s, 1), :].astype(F32)
        gate = n / (n + 8.0)
        full = jnp.where(spot == row, gate, 0.0)
        hi = full.astype(BF)
        lo = (full - hi.astype(F32)).astype(BF)
        values = fe[s, j]
        grid = mm(hi, values) + mm(lo, values) + emb[pl.ds(tile * nsweep + s, 1), :]
        mid = grid.astype(BF)
        grid = mid.astype(F32)
        left = jnp.where(col == 0, 0.0, pltpu.roll(grid, 1, 0)).astype(BF)
        right = jnp.where(col == W - 1, 0.0, pltpu.roll(grid, band - 1, 0)).astype(BF)
        rows = pl.ds(pl.multiple_of(W + j * band, W), band)
        x3[s, rows, 0:width] = left
        x3[s, rows, width:2 * width] = mid
        x3[s, rows, 2 * width:3 * width] = right

    for c in locals_[:6]:
        c.wait()
    for i in range(3):
        wqkv[:, i * width:(i + 1) * width] = proj[i, 0]
    emb[...] = embed[...].astype(F32)

    def own_band(s, c):
        grid_band(s, tile)
        return c

    lax.fori_loop(0, nsweep, own_band, 0, unroll=2)
    for d in range(1, nt):
        for k in range(3):
            arrival(k, peer(d)).wait_recv()
    for d in range(1, nt):
        outgoing(3, peer(d)).start()

    def forward(s, total):
        for d in range(1, nt):
            grid_band(s, peer(d))
        pre = mm(x3[s, 0:cells, :], wconv[0])
        pre = pre + mm(x3[s, W:W + cells, :], wconv[1])
        pre = pre + mm(x3[s, 2 * W:2 * W + cells, :], wconv[2])
        sig = 1.0 / (1.0 + jnp.exp(-pre))
        f = (pre * sig).astype(BF)
        feats[s] = f
        deriv[s] = sig * (1.0 + pre * (1.0 - sig))
        out = mm(f, wqkv[...]).astype(BF)
        qkv[s] = out
        total = total + mm(out[:, width:2 * width], out[:, 2 * width:], 0, 0)
        kvl[s] = total
        return total

    kv_total = lax.fori_loop(0, nsweep, forward, jnp.zeros((width, width), F32), unroll=2)

    def tile_copy(k, to, slot, sem):
        return pltpu.make_async_remote_copy(
            src_ref=tks.at[k], dst_ref=tkr.at[k, slot], send_sem=tk_s.at[k, to],
            recv_sem=tk_r.at[k, sem], device_id={"tile": to}, device_id_type=MESH,
        )

    def block_copy(k, to, slot, sem):
        return pltpu.make_async_remote_copy(
            src_ref=zks.at[k], dst_ref=zkr.at[k, slot], send_sem=zk_s.at[k, to],
            recv_sem=zk_r.at[k, sem], device_id={"tm": to}, device_id_type=MESH,
        )

    def send_tile(k, total):
        low = total.astype(BF)
        tks[k] = low
        tkr[k, tile] = low
        for d in range(1, nt):
            tile_copy(k, peer(d), tile, tile).start()

    def reaches(k, m):
        return (m > tm) if k == 0 else (m < tm)

    def send_block(k):
        for d in range(1, nt):
            tile_copy(k, peer(d), peer(d), peer(d)).wait_recv()
        block = jnp.zeros((width, width), F32)
        inside = jnp.zeros((width, width), F32)
        for i in range(nt):
            part = tkr[k, i].astype(F32)
            block = block + part
            wanted = (i < tile) if k == 0 else (i > tile)
            inside = inside + jnp.where(wanted, part, 0.0)
        zks[k] = block.astype(BF)
        for m in range(nm):
            @pl.when(reaches(k, m))
            def _():
                block_copy(k, m, tm, tm).start()
        return inside

    def take_block(k, inside):
        for m in range(nm):
            @pl.when(reaches(1 - k, m))
            def _():
                block_copy(k, m, m, m).wait_recv()
        for m in range(nm):
            inside = inside + zkr[k, m].astype(F32)
        return inside

    def scale_of(s):
        t = tm * (nsweep * nt) + tile * nsweep + s + 1
        return 1.0 / (jnp.full((1, width), t, jnp.int32).astype(F32) * float(cells))

    send_tile(0, kv_total)
    kv_inside = send_block(0)
    locals_[6].wait()
    for d in range(1, nt):
        arrival(3, peer(d)).wait_recv()

    def cot_sum(k, total):
        s = nsweep - 1 - k
        total = total + mm(qkv[s, :, 0:width], cot[s].reshape(cells, width), 0, 0) * scale_of(s)
        cotl[s] = total
        return total

    cot_total = lax.fori_loop(0, nsweep, cot_sum, jnp.zeros((width, width), F32), unroll=2)
    send_tile(1, cot_total)
    before = take_block(0, kv_inside)

    def attn_remote(s, to, slot):
        return pltpu.make_async_remote_copy(
            src_ref=ao.at[s, to], dst_ref=attn.at[slot * nsweep + s], send_sem=att_s.at[s, to],
            recv_sem=att_r.at[s, slot], device_id={"tile": to}, device_id_type=MESH,
        )

    def attn_local(s):
        return pltpu.make_async_copy(ao.at[s, tile], attn.at[tile * nsweep + s], att_l.at[s])

    def attend(s, c):
        state = (before + kvl[s]).astype(BF)
        res = mm(qkv[s, :, 0:width], state) * scale_of(s)
        ao[s] = res.astype(BF).reshape(nt, band, width)
        for d in range(1, nt):
            attn_remote(s, peer(d), tile).start()
        attn_local(s).start()
        gqs[s] = (mm(cot[s].reshape(cells, width), state, 1, 1) * scale_of(s)).astype(BF)
        return c

    cot_inside = send_block(1)
    lax.fori_loop(0, nsweep, attend, 0, unroll=2)
    after = take_block(1, cot_inside)

    def backward(s, c):
        adj = (after + cotl[s]).astype(BF)
        gk = mm(qkv[s, :, 2 * width:3 * width], adj, 1, 1).astype(BF)
        gv = mm(qkv[s, :, width:2 * width], adj).astype(BF)
        g = jnp.concatenate([gqs[s], gk, gv], axis=1)
        pacc[...] += mm(feats[s], g, 0, 0)
        gp = (mm(g, wqkv[...], 1, 1) * deriv[s]).astype(BF)
        slot = lax.rem(s, 2)
        g3[slot, 0:cells - W, 0:width] = gp[W:]
        g3[slot, :, width:2 * width] = gp
        g3[slot, W:cells, 2 * width:3 * width] = gp[:cells - W]
        cacc[...] += mm(x3[s, W:W + cells, :], g3[slot], 0, 0)
        return c

    lax.fori_loop(0, nsweep, backward, 0, unroll=2)

    nconv = 9 * width
    for a in range(3):
        for b in range(3):
            r = (3 * a + b) * width
            gflat[r:r + width] = cacc[b * width:(b + 1) * width, a * width:(a + 1) * width]
    for i in range(3):
        r = nconv + i * width
        gflat[r:r + width] = pacc[:, i * width:(i + 1) * width]
    extra = gflat.shape[0] - 12 * width
    if extra:
        gflat[12 * width:] = jnp.zeros((extra, width), F32)
    gsend[...] = gflat[...].astype(BF).reshape(gsend.shape)

    def part_copy(p, src, slot):
        return pltpu.make_async_remote_copy(
            src_ref=gsend.at[src], dst_ref=grecv.at[slot], send_sem=gs_s.at[p],
            recv_sem=gs_r.at[slot], device_id=gid(p), device_id_type=MESH,
        )

    def sum_copy(p, slot):
        return pltpu.make_async_remote_copy(
            src_ref=gall.at[slot], dst_ref=gall.at[slot], send_sem=ga_s.at[p],
            recv_sem=ga_r.at[slot], device_id=gid(p), device_id_type=MESH,
        )

    def each(fn, start=1):
        def step(d, c):
            fn(gpeer(d))
            return c
        lax.fori_loop(start, group, step, 0)

    each(lambda p: part_copy(p, p, me).start())

    def add_part(d, total):
        p = gpeer(d)
        part_copy(p, p, p).wait_recv()
        return total + grecv[p].astype(F32)

    total = lax.fori_loop(1, group, add_part, gsend[me].astype(F32))
    gall[me] = total.astype(BF)
    each(lambda p: sum_copy(p, me).start())
    each(lambda p: sum_copy(p, p).wait_recv())
    flat = gall[...].reshape(gflat.shape)
    gconv[...] = flat[0:nconv].astype(F32)
    gproj[...] = flat[nconv:12 * width].astype(F32)

    def drain(s, c):
        for d in range(1, nt):
            attn_remote(s, peer(d), tile).wait_send()
            attn_remote(s, peer(d), peer(d)).wait_recv()
        attn_local(s).wait()
        return c

    lax.fori_loop(0, nsweep, drain, 0)
    for d in range(1, nt):
        for k in range(4):
            outgoing(k, peer(d)).wait_send()
        for k in range(2):
            tile_copy(k, peer(d), tile, tile).wait_send()
    for k in range(2):
        for m in range(nm):
            @pl.when(reaches(k, m))
            def _():
                block_copy(k, m, tm, tm).wait_send()
    each(lambda p: part_copy(p, p, me).wait_send())
    each(lambda p: sum_copy(p, me).wait_send())


def local(nm, nt, feat, cell, count, embed, wconv, proj, dout):
    block, per_tile, width = feat.shape
    band = dout.shape[1]
    nsweep = block // nt
    cells = nt * band
    group = nm * nt
    piece = -(-12 * width // (16 * group)) * 16
    vm = pltpu.VMEM
    dma = pltpu.SemaphoreType.DMA
    vspec = pl.BlockSpec(memory_space=pltpu.VMEM)
    aspec = pl.BlockSpec(memory_space=pl.ANY)
    hspec = pl.BlockSpec(memory_space=pltpu.HBM)
    tokens = nsweep * cells
    out = pl.pallas_call(
        functools.partial(body, nm, nt, nsweep, per_tile, band),
        out_shape=(
            jax.ShapeDtypeStruct((block, band, width), BF),
            jax.ShapeDtypeStruct((9 * width, width), F32),
            jax.ShapeDtypeStruct((3 * width, width), F32),
        ),
        in_specs=[hspec] * 7,
        out_specs=(aspec, vspec, vspec),
        scratch_shapes=[
            vm((block, width), BF),
            vm((3, 3 * width, width), BF),
            vm((3, 1, width, width), BF),
            vm((nsweep, nt, per_tile, width), BF),
            vm((nt, nsweep, per_tile), jnp.int32),
            vm((nt, nsweep, per_tile), jnp.int32),
            vm((nsweep, nt, band, width), BF),
            vm((block, width), F32),
            vm((nsweep, cells + 2 * W, 3 * width), BF),
            vm((nsweep, cells, width), BF),
            vm((nsweep, cells, width), BF),
            vm((nsweep, cells, width), F32),
            vm((nsweep, cells, 3 * width), BF),
            vm((nsweep, width, width), F32),
            vm((nsweep, width, width), F32),
            vm((width, 3 * width), BF),
            vm((nsweep, nt, band, width), BF),
            vm((2, cells, 3 * width), BF),
            vm((3 * width, 3 * width), F32),
            vm((width, 3 * width), F32),
            vm((2, width, width), BF),
            vm((2, nt, width, width), BF),
            vm((2, width, width), BF),
            vm((2, nm, width, width), BF),
            vm((group * piece, width), F32),
            vm((group, piece, width), BF),
            vm((group, piece, width), BF),
            vm((group, piece, width), BF),
            dma((4, nt)), dma((4, nt)), dma((7,)),
            dma((2, nt)), dma((2, nt)), dma((2, nm)), dma((2, nm)),
            dma((nsweep, nt)), dma((nsweep, nt)), dma((nsweep,)),
            dma((group,)), dma((group,)), dma((group,)), dma((group,)),
        ],
        compiler_params=pltpu.CompilerParams(
            collective_id=0, has_side_effects=True, vmem_limit_bytes=65000 * 1024
        ),
        cost_estimate=pl.CostEstimate(
            flops=2 * tokens * width * width * 36, bytes_accessed=4 * 1024 * 1024,
            transcendentals=tokens * width,
        ),
    )(
        feat, cell.reshape(nt, nsweep, per_tile), count.reshape(nt, nsweep, per_tile),
        embed, wconv.reshape(3, 3 * width, width), proj, dout,
    )
    return (
        out[0],
        out[1].reshape(9, width, width),
        out[2].reshape(3, 1, width, width),
    )


def solution(mesh):
    return jax.shard_map(
        functools.partial(local, mesh.shape["tm"], mesh.shape["tile"]),
        mesh=mesh,
        in_specs=(
            P(("parts", "tm"), "tile", None),
            P(("parts", "tm"), "tile"),
            P(("parts", "tm"), "tile"),
            P(("parts", "tm"), None),
            P(None, None, "chan"),
            P(None, "chan", None, None),
            P(("parts", "tm"), "tile", "chan"),
        ),
        out_specs=(
            P(("parts", "tm"), "tile", "chan"),
            P(None, "parts", "chan"),
            P(None, "chan", "parts", None),
        ),
        check_vma=False,
    )
```

```python
import functools

import jax
import jax.numpy as jnp
from jax import lax
from jax.experimental import pallas as pl
from jax.experimental.pallas import tpu as pltpu
from jax.sharding import PartitionSpec as P

W = 64
BF = jnp.bfloat16
F32 = jnp.float32
MESH = pl.DeviceIdType.MESH


def mm(a, b, ca=1, cb=0):
    return lax.dot_general(a, b, (((ca,), (cb,)), ((), ())), preferred_element_type=F32)


def body(
    nm, nt, nsweep, per_tile, band,
    feat, cell, count, embed_in, wconv_in, proj_in, dout,
    attn, gconv, gproj,
    embed, wconv, proj, fe, ce, ne, cot, emb, x3, feats, gqs, deriv, qkv, kvl, cotl, wqkv, ao, g3, cacc, pacc,
    tks, tkr, zks, zkr, gflats, gsends, grecvs, galls,
    pil_s, pil_r, loc, tk_s, tk_r, zk_s, zk_r, att_s, att_r, att_l, gs_s, gs_r, ga_s, ga_r,
):
    group = nm * nt
    cells = nt * band
    width = 128
    tm = lax.axis_index("tm")
    tile = lax.axis_index("tile")
    me = tm * nt + tile

    def peer(d):
        return lax.rem(tile + d, nt)

    def gpeer(d):
        return lax.rem(me + d, group)

    def gid(p):
        return {"tm": p // nt, "tile": lax.rem(p, nt)}

    zkr[...] = jnp.zeros_like(zkr)

    barrier = pltpu.get_barrier_semaphore()

    def greet(d, c):
        pl.semaphore_signal(barrier, inc=1, device_id=gid(gpeer(d)), device_id_type=MESH)
        return c

    lax.fori_loop(1, group, greet, 0)
    mine = pl.ds(tile * nsweep, nsweep)
    locals_ = [
        pltpu.make_async_copy(feat.at[mine], fe.at[:, tile], loc.at[0]),
        pltpu.make_async_copy(cell.at[tile], ce.at[tile], loc.at[1]),
        pltpu.make_async_copy(count.at[tile], ne.at[tile], loc.at[2]),
        pltpu.make_async_copy(embed_in, embed, loc.at[3]),
        pltpu.make_async_copy(wconv_in, wconv, loc.at[4]),
        pltpu.make_async_copy(proj_in, proj, loc.at[5]),
        pltpu.make_async_copy(dout.at[mine], cot.at[:, tile], loc.at[6]),
    ]
    for c in locals_:
        c.start()
    edge = jnp.zeros((nsweep, W, 3 * width), BF)
    x3[:, 0:W, :] = edge
    x3[:, W + cells:2 * W + cells, :] = edge
    g3[:, cells - W:cells, 0:width] = edge[:, :, 0:width]
    g3[:, 0:W, 2 * width:3 * width] = edge[:, :, 0:width]
    cacc[...] = jnp.zeros_like(cacc)
    pacc[...] = jnp.zeros_like(pacc)
    pl.semaphore_wait(barrier, group - 1)

    def pillar_copy(k, to, here, slot):
        theirs = pl.ds(here * nsweep, nsweep)
        src, dst = (
            lambda: (feat.at[theirs], fe.at[:, slot]),
            lambda: (cell.at[here], ce.at[slot]),
            lambda: (count.at[here], ne.at[slot]),
            lambda: (dout.at[theirs], cot.at[:, slot]),
        )[k]()
        return pltpu.make_async_remote_copy(
            src_ref=src, dst_ref=dst, send_sem=pil_s.at[k, to], recv_sem=pil_r.at[k, slot],
            device_id={"tile": to}, device_id_type=MESH,
        )

    def outgoing(k, to):
        return pillar_copy(k, to, to, tile)

    def arrival(k, frm):
        return pillar_copy(k, frm, tile, frm)

    for d in range(1, nt):
        for k in range(3):
            outgoing(k, peer(d)).start()


    spot = lax.broadcasted_iota(jnp.int32, (band, per_tile), 0)
    col = lax.rem(lax.broadcasted_iota(jnp.int32, (band, width), 0), W)

    def grid_band(s, j):
        row = ce[j, pl.ds(s, 1), :]
        n = ne[j, pl.ds(s, 1), :].astype(F32)
        gate = n / (n + 8.0)
        full = jnp.where(spot == row, gate, 0.0)
        hi = full.astype(BF)
        lo = (full - hi.astype(F32)).astype(BF)
        values = fe[s, j]
        grid = mm(hi, values) + mm(lo, values) + emb[pl.ds(tile * nsweep + s, 1), :]
        mid = grid.astype(BF)
        grid = mid.astype(F32)
        left = jnp.where(col == 0, 0.0, pltpu.roll(grid, 1, 0)).astype(BF)
        right = jnp.where(col == W - 1, 0.0, pltpu.roll(grid, band - 1, 0)).astype(BF)
        rows = pl.ds(pl.multiple_of(W + j * band, W), band)
        x3[s, rows, 0:width] = left
        x3[s, rows, width:2 * width] = mid
        x3[s, rows, 2 * width:3 * width] = right

    for c in locals_[:6]:
        c.wait()
    for i in range(3):
        wqkv[:, i * width:(i + 1) * width] = proj[i, 0]
    emb[...] = embed[...].astype(F32)

    def own_band(s, c):
        grid_band(s, tile)
        return c

    lax.fori_loop(0, nsweep, own_band, 0, unroll=2)
    for d in range(1, nt):
        for k in range(3):
            arrival(k, peer(d)).wait_recv()
    for d in range(1, nt):
        outgoing(3, peer(d)).start()

    def forward(s, total):
        for d in range(1, nt):
            grid_band(s, peer(d))
        pre = mm(x3[s, 0:cells, :], wconv[0])
        pre = pre + mm(x3[s, W:W + cells, :], wconv[1])
        pre = pre + mm(x3[s, 2 * W:2 * W + cells, :], wconv[2])
        sig = 1.0 / (1.0 + jnp.exp(-pre))
        f = (pre * sig).astype(BF)
        feats[s] = f
        deriv[s] = sig * (1.0 + pre * (1.0 - sig))
        out = mm(f, wqkv[...]).astype(BF)
        qkv[s] = out
        total = total + mm(out[:, width:2 * width], out[:, 2 * width:], 0, 0)
        kvl[s] = total
        return total

    kv_total = lax.fori_loop(0, nsweep, forward, jnp.zeros((width, width), F32), unroll=2)

    def tile_copy(k, to, slot, sem):
        return pltpu.make_async_remote_copy(
            src_ref=tks.at[k], dst_ref=tkr.at[k, slot], send_sem=tk_s.at[k, to],
            recv_sem=tk_r.at[k, sem], device_id={"tile": to}, device_id_type=MESH,
        )

    def block_copy(k, to, slot, sem):
        return pltpu.make_async_remote_copy(
            src_ref=zks.at[k], dst_ref=zkr.at[k, slot], send_sem=zk_s.at[k, to],
            recv_sem=zk_r.at[k, sem], device_id={"tm": to}, device_id_type=MESH,
        )

    def send_tile(k, total):
        low = total.astype(BF)
        tks[k] = low
        tkr[k, tile] = low
        for d in range(1, nt):
            tile_copy(k, peer(d), tile, tile).start()

    def reaches(k, m):
        return (m > tm) if k == 0 else (m < tm)

    def send_block(k):
        for d in range(1, nt):
            tile_copy(k, peer(d), peer(d), peer(d)).wait_recv()
        block = jnp.zeros((width, width), F32)
        inside = jnp.zeros((width, width), F32)
        for i in range(nt):
            part = tkr[k, i].astype(F32)
            block = block + part
            wanted = (i < tile) if k == 0 else (i > tile)
            inside = inside + jnp.where(wanted, part, 0.0)
        zks[k] = block.astype(BF)
        for m in range(nm):
            @pl.when(reaches(k, m))
            def _():
                block_copy(k, m, tm, tm).start()
        return inside

    def take_block(k, inside):
        for m in range(nm):
            @pl.when(reaches(1 - k, m))
            def _():
                block_copy(k, m, m, m).wait_recv()
        for m in range(nm):
            inside = inside + zkr[k, m].astype(F32)
        return inside

    def scale_of(s):
        t = tm * (nsweep * nt) + tile * nsweep + s + 1
        return 1.0 / (jnp.full((1, width), t, jnp.int32).astype(F32) * float(cells))

    send_tile(0, kv_total)
    kv_inside = send_block(0)
    locals_[6].wait()
    for d in range(1, nt):
        arrival(3, peer(d)).wait_recv()

    def cot_sum(k, total):
        s = nsweep - 1 - k
        total = total + mm(qkv[s, :, 0:width], cot[s].reshape(cells, width), 0, 0) * scale_of(s)
        cotl[s] = total
        return total

    cot_total = lax.fori_loop(0, nsweep, cot_sum, jnp.zeros((width, width), F32), unroll=2)
    send_tile(1, cot_total)
    before = take_block(0, kv_inside)

    def attn_remote(s, to, slot):
        return pltpu.make_async_remote_copy(
            src_ref=ao.at[s, to], dst_ref=attn.at[slot * nsweep + s], send_sem=att_s.at[s, to],
            recv_sem=att_r.at[s, slot], device_id={"tile": to}, device_id_type=MESH,
        )

    def attn_local(s):
        return pltpu.make_async_copy(ao.at[s, tile], attn.at[tile * nsweep + s], att_l.at[s])

    def attend(s, c):
        state = (before + kvl[s]).astype(BF)
        res = mm(qkv[s, :, 0:width], state) * scale_of(s)
        ao[s] = res.astype(BF).reshape(nt, band, width)
        for d in range(1, nt):
            attn_remote(s, peer(d), tile).start()
        attn_local(s).start()
        gqs[s] = (mm(cot[s].reshape(cells, width), state, 1, 1) * scale_of(s)).astype(BF)
        return c

    cot_inside = send_block(1)
    lax.fori_loop(0, nsweep, attend, 0, unroll=2)
    after = take_block(1, cot_inside)

    def backward(s, c):
        adj = (after + cotl[s]).astype(BF)
        gk = mm(qkv[s, :, 2 * width:3 * width], adj, 1, 1).astype(BF)
        gv = mm(qkv[s, :, width:2 * width], adj).astype(BF)
        g = jnp.concatenate([gqs[s], gk, gv], axis=1)
        pacc[...] += mm(feats[s], g, 0, 0)
        gp = (mm(g, wqkv[...], 1, 1) * deriv[s]).astype(BF)
        g3[s, 0:cells - W, 0:width] = gp[W:]
        g3[s, :, width:2 * width] = gp
        g3[s, W:cells, 2 * width:3 * width] = gp[:cells - W]
        return c

    def conv_part(s, c):
        cacc[...] += mm(x3[s, W:W + cells, :], g3[s], 0, 0)
        return c

    lax.fori_loop(0, nsweep, backward, 0, unroll=2)

    def part_copy(k, p, src, slot):
        return pltpu.make_async_remote_copy(
            src_ref=gsends[k].at[src], dst_ref=grecvs[k].at[slot], send_sem=gs_s.at[k, p],
            recv_sem=gs_r.at[k, slot], device_id=gid(p), device_id_type=MESH,
        )

    def sum_copy(k, p, slot):
        return pltpu.make_async_remote_copy(
            src_ref=galls[k].at[slot], dst_ref=galls[k].at[slot], send_sem=ga_s.at[k, p],
            recv_sem=ga_r.at[k, slot], device_id=gid(p), device_id_type=MESH,
        )

    def each(fn):
        def step(d, c):
            fn(gpeer(d))
            return c
        lax.fori_loop(1, group, step, 0)

    def send_parts(k, blocks):
        gflat = gflats[k]
        for i, block in enumerate(blocks):
            gflat[i * width:(i + 1) * width] = block
        used = len(blocks) * width
        if gflat.shape[0] > used:
            gflat[used:] = jnp.zeros((gflat.shape[0] - used, width), F32)
        gsends[k][...] = gflat[...].astype(BF).reshape(gsends[k].shape)
        each(lambda p: part_copy(k, p, p, me).start())

    def send_sums(k):
        def add_part(d, total):
            p = gpeer(d)
            part_copy(k, p, p, p).wait_recv()
            return total + grecvs[k][p].astype(F32)

        total = lax.fori_loop(1, group, add_part, gsends[k][me].astype(F32))
        galls[k][me] = total.astype(BF)
        each(lambda p: sum_copy(k, p, me).start())

    def finish(k, out):
        each(lambda p: sum_copy(k, p, p).wait_recv())
        flat = galls[k][...].reshape(gflats[k].shape)
        out[...] = flat[0:out.shape[0]].astype(F32)

    send_parts(0, [pacc[:, i * width:(i + 1) * width] for i in range(3)])
    half = nsweep // 2
    lax.fori_loop(0, half, conv_part, 0, unroll=min(2, max(half, 1)))
    send_sums(0)
    lax.fori_loop(half, nsweep, conv_part, 0, unroll=min(2, nsweep - half))
    send_parts(1, [
        cacc[b * width:(b + 1) * width, a * width:(a + 1) * width]
        for a in range(3) for b in range(3)
    ])
    finish(0, gproj)
    send_sums(1)
    finish(1, gconv)

    def drain(s, c):
        for d in range(1, nt):
            attn_remote(s, peer(d), tile).wait_send()
            attn_remote(s, peer(d), peer(d)).wait_recv()
        attn_local(s).wait()
        return c

    lax.fori_loop(0, nsweep, drain, 0)
    for d in range(1, nt):
        for k in range(4):
            outgoing(k, peer(d)).wait_send()
        for k in range(2):
            tile_copy(k, peer(d), tile, tile).wait_send()
    for k in range(2):
        for m in range(nm):
            @pl.when(reaches(k, m))
            def _():
                block_copy(k, m, tm, tm).wait_send()
    for k in range(2):
        each(lambda p: part_copy(k, p, p, me).wait_send())
        each(lambda p: sum_copy(k, p, me).wait_send())


def local(nm, nt, feat, cell, count, embed, wconv, proj, dout):
    block, per_tile, width = feat.shape
    band = dout.shape[1]
    nsweep = block // nt
    cells = nt * band
    group = nm * nt
    pieces = [-(-n * width // (16 * group)) * 16 for n in (3, 9)]
    vm = pltpu.VMEM
    dma = pltpu.SemaphoreType.DMA
    vspec = pl.BlockSpec(memory_space=pltpu.VMEM)
    aspec = pl.BlockSpec(memory_space=pl.ANY)
    hspec = pl.BlockSpec(memory_space=pltpu.HBM)
    tokens = nsweep * cells
    out = pl.pallas_call(
        functools.partial(body, nm, nt, nsweep, per_tile, band),
        out_shape=(
            jax.ShapeDtypeStruct((block, band, width), BF),
            jax.ShapeDtypeStruct((9 * width, width), F32),
            jax.ShapeDtypeStruct((3 * width, width), F32),
        ),
        in_specs=[hspec] * 7,
        out_specs=(aspec, vspec, vspec),
        scratch_shapes=[
            vm((block, width), BF),
            vm((3, 3 * width, width), BF),
            vm((3, 1, width, width), BF),
            vm((nsweep, nt, per_tile, width), BF),
            vm((nt, nsweep, per_tile), jnp.int32),
            vm((nt, nsweep, per_tile), jnp.int32),
            vm((nsweep, nt, band, width), BF),
            vm((block, width), F32),
            vm((nsweep, cells + 2 * W, 3 * width), BF),
            vm((nsweep, cells, width), BF),
            vm((nsweep, cells, width), BF),
            vm((nsweep, cells, width), F32),
            vm((nsweep, cells, 3 * width), BF),
            vm((nsweep, width, width), F32),
            vm((nsweep, width, width), F32),
            vm((width, 3 * width), BF),
            vm((nsweep, nt, band, width), BF),
            vm((nsweep, cells, 3 * width), BF),
            vm((3 * width, 3 * width), F32),
            vm((width, 3 * width), F32),
            vm((2, width, width), BF),
            vm((2, nt, width, width), BF),
            vm((2, width, width), BF),
            vm((2, nm, width, width), BF),
            [vm((group * p, width), F32) for p in pieces],
            [vm((group, p, width), BF) for p in pieces],
            [vm((group, p, width), BF) for p in pieces],
            [vm((group, p, width), BF) for p in pieces],
            dma((4, nt)), dma((4, nt)), dma((7,)),
            dma((2, nt)), dma((2, nt)), dma((2, nm)), dma((2, nm)),
            dma((nsweep, nt)), dma((nsweep, nt)), dma((nsweep,)),
            dma((2, group)), dma((2, group)), dma((2, group)), dma((2, group)),
        ],
        compiler_params=pltpu.CompilerParams(
            collective_id=0, has_side_effects=True, vmem_limit_bytes=65000 * 1024
        ),
        cost_estimate=pl.CostEstimate(
            flops=2 * tokens * width * width * 36, bytes_accessed=4 * 1024 * 1024,
            transcendentals=tokens * width,
        ),
    )(
        feat, cell.reshape(nt, nsweep, per_tile), count.reshape(nt, nsweep, per_tile),
        embed, wconv.reshape(3, 3 * width, width), proj, dout,
    )
    return (
        out[0],
        out[1].reshape(9, width, width),
        out[2].reshape(3, 1, width, width),
    )


def solution(mesh):
    return jax.shard_map(
        functools.partial(local, mesh.shape["tm"], mesh.shape["tile"]),
        mesh=mesh,
        in_specs=(
            P(("parts", "tm"), "tile", None),
            P(("parts", "tm"), "tile"),
            P(("parts", "tm"), "tile"),
            P(("parts", "tm"), None),
            P(None, None, "chan"),
            P(None, "chan", None, None),
            P(("parts", "tm"), "tile", "chan"),
        ),
        out_specs=(
            P(("parts", "tm"), "tile", "chan"),
            P(None, "parts", "chan"),
            P(None, "chan", "parts", None),
        ),
        check_vma=False,
    )
```

```python
import functools

import jax
import jax.numpy as jnp
from jax import lax
from jax.experimental import pallas as pl
from jax.experimental.pallas import tpu as pltpu
from jax.sharding import PartitionSpec as P

W = 64
BF = jnp.bfloat16
F32 = jnp.float32
MESH = pl.DeviceIdType.MESH


def mm(a, b, ca=1, cb=0):
    return lax.dot_general(a, b, (((ca,), (cb,)), ((), ())), preferred_element_type=F32)


def body(
    nm, nt, nsweep, per_tile, band,
    feat, cell, count, embed_in, wconv_in, proj_in, dout,
    attn, gconv, gproj,
    embed, wconv, proj, fe, ce, ne, cot, emb, x3, feats, gqs, deriv, qkv, kvl, cotl, wqkv, ao, g3, cacc, pacc,
    tks, tkr, zks, zkr, gflat, gsend, grecv, gall,
    pil_s, pil_r, loc, tk_s, tk_r, zk_s, zk_r, att_s, att_r, att_l, gs_s, gs_r, ga_s, ga_r,
):
    group = nm * nt
    cells = nt * band
    width = 128
    tm = lax.axis_index("tm")
    tile = lax.axis_index("tile")
    me = tm * nt + tile

    def peer(d):
        return lax.rem(tile + d, nt)

    def gpeer(d):
        return lax.rem(me + d, group)

    def gid(p):
        return {"tm": p // nt, "tile": lax.rem(p, nt)}

    zkr[...] = jnp.zeros_like(zkr)

    barrier = pltpu.get_barrier_semaphore()

    def greet(d, c):
        pl.semaphore_signal(barrier, inc=1, device_id=gid(gpeer(d)), device_id_type=MESH)
        return c

    lax.fori_loop(1, group, greet, 0)
    mine = pl.ds(tile * nsweep, nsweep)
    locals_ = [
        pltpu.make_async_copy(feat.at[mine], fe.at[:, tile], loc.at[0]),
        pltpu.make_async_copy(cell.at[tile], ce.at[tile], loc.at[1]),
        pltpu.make_async_copy(count.at[tile], ne.at[tile], loc.at[2]),
        pltpu.make_async_copy(embed_in, embed, loc.at[3]),
        pltpu.make_async_copy(wconv_in, wconv, loc.at[4]),
        pltpu.make_async_copy(proj_in, proj, loc.at[5]),
        pltpu.make_async_copy(dout.at[mine], cot.at[:, tile], loc.at[6]),
    ]
    for c in locals_:
        c.start()
    edge = jnp.zeros((nsweep, W, 3 * width), BF)
    x3[:, 0:W, :] = edge
    x3[:, W + cells:2 * W + cells, :] = edge
    g3[...] = jnp.zeros_like(g3)
    cacc[...] = jnp.zeros_like(cacc)
    pacc[...] = jnp.zeros_like(pacc)
    pl.semaphore_wait(barrier, group - 1)

    def pillar_copy(k, to, here, slot):
        theirs = pl.ds(here * nsweep, nsweep)
        src, dst = (
            lambda: (feat.at[theirs], fe.at[:, slot]),
            lambda: (cell.at[here], ce.at[slot]),
            lambda: (count.at[here], ne.at[slot]),
            lambda: (dout.at[theirs], cot.at[:, slot]),
        )[k]()
        return pltpu.make_async_remote_copy(
            src_ref=src, dst_ref=dst, send_sem=pil_s.at[k, to], recv_sem=pil_r.at[k, slot],
            device_id={"tile": to}, device_id_type=MESH,
        )

    def outgoing(k, to):
        return pillar_copy(k, to, to, tile)

    def arrival(k, frm):
        return pillar_copy(k, frm, tile, frm)

    for d in range(1, nt):
        for k in range(3):
            outgoing(k, peer(d)).start()


    spot = lax.broadcasted_iota(jnp.int32, (band, per_tile), 0)
    col = lax.rem(lax.broadcasted_iota(jnp.int32, (band, width), 0), W)

    def grid_band(s, j):
        row = ce[j, pl.ds(s, 1), :]
        n = ne[j, pl.ds(s, 1), :].astype(F32)
        gate = n / (n + 8.0)
        full = jnp.where(spot == row, gate, 0.0)
        hi = full.astype(BF)
        lo = (full - hi.astype(F32)).astype(BF)
        values = fe[s, j]
        grid = mm(hi, values) + mm(lo, values) + emb[pl.ds(tile * nsweep + s, 1), :]
        mid = grid.astype(BF)
        grid = mid.astype(F32)
        left = jnp.where(col == 0, 0.0, pltpu.roll(grid, 1, 0)).astype(BF)
        right = jnp.where(col == W - 1, 0.0, pltpu.roll(grid, band - 1, 0)).astype(BF)
        rows = pl.ds(pl.multiple_of(W + j * band, W), band)
        x3[s, rows, 0:width] = left
        x3[s, rows, width:2 * width] = mid
        x3[s, rows, 2 * width:3 * width] = right

    for c in locals_[:6]:
        c.wait()
    for i in range(3):
        wqkv[:, i * width:(i + 1) * width] = proj[i, 0]
    emb[...] = embed[...].astype(F32)

    def own_band(s, c):
        grid_band(s, tile)
        return c

    lax.fori_loop(0, nsweep, own_band, 0, unroll=min(4, nsweep))
    for d in range(1, nt):
        for k in range(3):
            arrival(k, peer(d)).wait_recv()
    for d in range(1, nt):
        outgoing(3, peer(d)).start()

    def forward(s, total):
        for d in range(1, nt):
            grid_band(s, peer(d))
        pre = mm(x3[s, 0:cells, :], wconv[0])
        pre = pre + mm(x3[s, W:W + cells, :], wconv[1])
        pre = pre + mm(x3[s, 2 * W:2 * W + cells, :], wconv[2])
        sig = 1.0 / (1.0 + jnp.exp(-pre))
        f = (pre * sig).astype(BF)
        feats[s] = f
        deriv[s] = sig * (1.0 + pre * (1.0 - sig))
        out = mm(f, wqkv[...]).astype(BF)
        qkv[s] = out
        total = total + mm(out[:, width:2 * width], out[:, 2 * width:], 0, 0)
        kvl[s] = total
        return total

    kv_total = lax.fori_loop(0, nsweep, forward, jnp.zeros((width, width), F32), unroll=min(4, nsweep))

    def tile_copy(k, to, slot, sem):
        return pltpu.make_async_remote_copy(
            src_ref=tks.at[k], dst_ref=tkr.at[k, slot], send_sem=tk_s.at[k, to],
            recv_sem=tk_r.at[k, sem], device_id={"tile": to}, device_id_type=MESH,
        )

    def block_copy(k, to, slot, sem):
        return pltpu.make_async_remote_copy(
            src_ref=zks.at[k], dst_ref=zkr.at[k, slot], send_sem=zk_s.at[k, to],
            recv_sem=zk_r.at[k, sem], device_id={"tm": to}, device_id_type=MESH,
        )

    def send_tile(k, total):
        low = total.astype(BF)
        tks[k] = low
        tkr[k, tile] = low
        for d in range(1, nt):
            tile_copy(k, peer(d), tile, tile).start()

    def reaches(k, m):
        return (m > tm) if k == 0 else (m < tm)

    def send_block(k):
        for d in range(1, nt):
            tile_copy(k, peer(d), peer(d), peer(d)).wait_recv()
        block = jnp.zeros((width, width), F32)
        inside = jnp.zeros((width, width), F32)
        for i in range(nt):
            part = tkr[k, i].astype(F32)
            block = block + part
            wanted = (i < tile) if k == 0 else (i > tile)
            inside = inside + jnp.where(wanted, part, 0.0)
        zks[k] = block.astype(BF)
        for m in range(nm):
            @pl.when(reaches(k, m))
            def _():
                block_copy(k, m, tm, tm).start()
        return inside

    def take_block(k, inside):
        for m in range(nm):
            @pl.when(reaches(1 - k, m))
            def _():
                block_copy(k, m, m, m).wait_recv()
        for m in range(nm):
            inside = inside + zkr[k, m].astype(F32)
        return inside

    def scale_of(s):
        t = tm * (nsweep * nt) + tile * nsweep + s + 1
        return 1.0 / (jnp.full((1, width), t, jnp.int32).astype(F32) * float(cells))

    send_tile(0, kv_total)
    kv_inside = send_block(0)
    locals_[6].wait()
    for d in range(1, nt):
        arrival(3, peer(d)).wait_recv()

    def cot_sum(k, total):
        s = nsweep - 1 - k
        total = total + mm(qkv[s, :, 0:width], cot[s].reshape(cells, width), 0, 0) * scale_of(s)
        cotl[s] = total
        return total

    cot_total = lax.fori_loop(0, nsweep, cot_sum, jnp.zeros((width, width), F32), unroll=min(4, nsweep))
    send_tile(1, cot_total)
    before = take_block(0, kv_inside)

    def attn_remote(s, to, slot):
        return pltpu.make_async_remote_copy(
            src_ref=ao.at[s, to], dst_ref=attn.at[slot * nsweep + s], send_sem=att_s.at[s, to],
            recv_sem=att_r.at[s, slot], device_id={"tile": to}, device_id_type=MESH,
        )

    def attn_local(s):
        return pltpu.make_async_copy(ao.at[s, tile], attn.at[tile * nsweep + s], att_l.at[s])

    def attend(s, c):
        state = (before + kvl[s]).astype(BF)
        res = mm(qkv[s, :, 0:width], state) * scale_of(s)
        ao[s] = res.astype(BF).reshape(nt, band, width)
        for d in range(1, nt):
            attn_remote(s, peer(d), tile).start()
        attn_local(s).start()
        gqs[s] = (mm(cot[s].reshape(cells, width), state, 1, 1) * scale_of(s)).astype(BF)
        return c

    cot_inside = send_block(1)
    lax.fori_loop(0, nsweep, attend, 0, unroll=min(4, nsweep))
    after = take_block(1, cot_inside)

    def backward(s, c):
        adj = (after + cotl[s]).astype(BF)
        gk = mm(qkv[s, :, 2 * width:3 * width], adj, 1, 1).astype(BF)
        gv = mm(qkv[s, :, width:2 * width], adj).astype(BF)
        g = jnp.concatenate([gqs[s], gk, gv], axis=1)
        pacc[...] += mm(feats[s], g, 0, 0)
        gp = (mm(g, wqkv[...], 1, 1) * deriv[s]).astype(BF)
        slot = lax.rem(s, 2)
        g3[slot, 0:cells - W, 0:width] = gp[W:]
        g3[slot, :, width:2 * width] = gp
        g3[slot, W:cells, 2 * width:3 * width] = gp[:cells - W]
        cacc[...] += mm(x3[s, W:W + cells, :], g3[slot], 0, 0)
        return c

    lax.fori_loop(0, nsweep, backward, 0, unroll=min(4, nsweep))

    nconv = 9 * width
    for a in range(3):
        for b in range(3):
            r = (3 * a + b) * width
            gflat[r:r + width] = cacc[b * width:(b + 1) * width, a * width:(a + 1) * width]
    for i in range(3):
        r = nconv + i * width
        gflat[r:r + width] = pacc[:, i * width:(i + 1) * width]
    extra = gflat.shape[0] - 12 * width
    if extra:
        gflat[12 * width:] = jnp.zeros((extra, width), F32)
    gsend[...] = gflat[...].astype(BF).reshape(gsend.shape)

    def part_copy(p, src, slot):
        return pltpu.make_async_remote_copy(
            src_ref=gsend.at[src], dst_ref=grecv.at[slot], send_sem=gs_s.at[p],
            recv_sem=gs_r.at[slot], device_id=gid(p), device_id_type=MESH,
        )

    def sum_copy(p, slot):
        return pltpu.make_async_remote_copy(
            src_ref=gall.at[slot], dst_ref=gall.at[slot], send_sem=ga_s.at[p],
            recv_sem=ga_r.at[slot], device_id=gid(p), device_id_type=MESH,
        )

    def each(fn, start=1):
        def step(d, c):
            fn(gpeer(d))
            return c
        lax.fori_loop(start, group, step, 0)

    each(lambda p: part_copy(p, p, me).start())

    def add_part(d, total):
        p = gpeer(d)
        part_copy(p, p, p).wait_recv()
        return total + grecv[p].astype(F32)

    total = lax.fori_loop(1, group, add_part, gsend[me].astype(F32))
    gall[me] = total.astype(BF)
    each(lambda p: sum_copy(p, me).start())
    each(lambda p: sum_copy(p, p).wait_recv())
    flat = gall[...].reshape(gflat.shape)
    gconv[...] = flat[0:nconv]
    gproj[...] = flat[nconv:12 * width]

    def drain(s, c):
        for d in range(1, nt):
            attn_remote(s, peer(d), tile).wait_send()
            attn_remote(s, peer(d), peer(d)).wait_recv()
        attn_local(s).wait()
        return c

    lax.fori_loop(0, nsweep, drain, 0)
    for d in range(1, nt):
        for k in range(4):
            outgoing(k, peer(d)).wait_send()
        for k in range(2):
            tile_copy(k, peer(d), tile, tile).wait_send()
    for k in range(2):
        for m in range(nm):
            @pl.when(reaches(k, m))
            def _():
                block_copy(k, m, tm, tm).wait_send()
    each(lambda p: part_copy(p, p, me).wait_send())
    each(lambda p: sum_copy(p, me).wait_send())


def local(nm, nt, feat, cell, count, embed, wconv, proj, dout):
    block, per_tile, width = feat.shape
    band = dout.shape[1]
    nsweep = block // nt
    cells = nt * band
    group = nm * nt
    piece = -(-12 * width // (16 * group)) * 16
    vm = pltpu.VMEM
    dma = pltpu.SemaphoreType.DMA
    vspec = pl.BlockSpec(memory_space=pltpu.VMEM)
    aspec = pl.BlockSpec(memory_space=pl.ANY)
    hspec = pl.BlockSpec(memory_space=pltpu.HBM)
    tokens = nsweep * cells
    out = pl.pallas_call(
        functools.partial(body, nm, nt, nsweep, per_tile, band),
        out_shape=(
            jax.ShapeDtypeStruct((block, band, width), BF),
            jax.ShapeDtypeStruct((9 * width, width), BF),
            jax.ShapeDtypeStruct((3 * width, width), BF),
        ),
        in_specs=[hspec] * 7,
        out_specs=(aspec, vspec, vspec),
        scratch_shapes=[
            vm((block, width), BF),
            vm((3, 3 * width, width), BF),
            vm((3, 1, width, width), BF),
            vm((nsweep, nt, per_tile, width), BF),
            vm((nt, nsweep, per_tile), jnp.int32),
            vm((nt, nsweep, per_tile), jnp.int32),
            vm((nsweep, nt, band, width), BF),
            vm((block, width), F32),
            vm((nsweep, cells + 2 * W, 3 * width), BF),
            vm((nsweep, cells, width), BF),
            vm((nsweep, cells, width), BF),
            vm((nsweep, cells, width), F32),
            vm((nsweep, cells, 3 * width), BF),
            vm((nsweep, width, width), F32),
            vm((nsweep, width, width), F32),
            vm((width, 3 * width), BF),
            vm((nsweep, nt, band, width), BF),
            vm((2, cells, 3 * width), BF),
            vm((3 * width, 3 * width), F32),
            vm((width, 3 * width), F32),
            vm((2, width, width), BF),
            vm((2, nt, width, width), BF),
            vm((2, width, width), BF),
            vm((2, nm, width, width), BF),
            vm((group * piece, width), F32),
            vm((group, piece, width), BF),
            vm((group, piece, width), BF),
            vm((group, piece, width), BF),
            dma((4, nt)), dma((4, nt)), dma((7,)),
            dma((2, nt)), dma((2, nt)), dma((2, nm)), dma((2, nm)),
            dma((nsweep, nt)), dma((nsweep, nt)), dma((nsweep,)),
            dma((group,)), dma((group,)), dma((group,)), dma((group,)),
        ],
        compiler_params=pltpu.CompilerParams(
            collective_id=0, has_side_effects=True, vmem_limit_bytes=65000 * 1024
        ),
        cost_estimate=pl.CostEstimate(
            flops=2 * tokens * width * width * 36, bytes_accessed=4 * 1024 * 1024,
            transcendentals=tokens * width,
        ),
    )(
        feat, cell.reshape(nt, nsweep, per_tile), count.reshape(nt, nsweep, per_tile),
        embed, wconv.reshape(3, 3 * width, width), proj, dout,
    )
    return (
        out[0],
        out[1].reshape(9, width, width).astype(F32),
        out[2].reshape(3, 1, width, width).astype(F32),
    )


def solution(mesh):
    return jax.shard_map(
        functools.partial(local, mesh.shape["tm"], mesh.shape["tile"]),
        mesh=mesh,
        in_specs=(
            P(("parts", "tm"), "tile", None),
            P(("parts", "tm"), "tile"),
            P(("parts", "tm"), "tile"),
            P(("parts", "tm"), None),
            P(None, None, "chan"),
            P(None, "chan", None, None),
            P(("parts", "tm"), "tile", "chan"),
        ),
        out_specs=(
            P(("parts", "tm"), "tile", "chan"),
            P(None, "parts", "chan"),
            P(None, "chan", "parts", None),
        ),
        check_vma=False,
    )
```
